512 devices in a mesh: dp: 32 (over x, z_hi, y), tensor: 16 (over z_lo, core).
Axes of the slice: x: 4, y: 4, z: 16 (z_hi: 2, z_lo: 8; z = z_hi * 8 + z_lo), core: 2. Of those that a mesh axis runs over, the one named last changes fastest.
Arguments:
- grad_hidden: bfloat16 [131072, 4096], P(('dp', 'tensor')), may hold values from -6 to 6
- positions: int32 [16384], P(('dp', 'tensor')), may hold values from 0 to 255, as said below
- owner_ids: int32 [16384, 1], P(('dp', 'tensor')), may hold values from 0 to 31; in each aligned block of 32 rows (0 to 31, 32 to 63, ...) at most 2 rows name the same one
- w_proj: bfloat16 [4608, 4096], P('tensor', 'dp'), may hold values from -0.09375 to 0.09375
- pre_act: bfloat16 [32, 1024, 4608], P('dp', None, 'tensor'), may hold values from -5 to 5
Outputs:
- grad_pre: bfloat16 [32, 1024, 4608], P('dp', None, 'tensor')
The draws below stay inside these ranges and needn't reach their ends.
Inputs may be any that keep to these rules, and one draw needn't show every extreme that they name: Within each aligned block of 32 entries (one device's image tokens) the positions are distinct and increasing. `owner_ids`: among the 32 image tokens of one device, at most 2 name the same owner.
All inputs are finite; a program needn't handle non-finite values.
Results may differ from the reference program's by a relative error of at most 0.001.
Values may be sent and summed in bfloat16 or wider, within the bound.
No kernel may reach another device: no remote copies, remote signals or barrier semaphores. Data moves between devices by JAX's collectives and lax.ppermute only.
A program may use at most 64 MiB of HBM per device.

```python
import math
import jax
import jax.numpy as jnp
import numpy as np

D = 4096
HID = 4608
TOK_DEV = 256
IMG_DEV = 32
CAP = 2
SLOTS = 1024
OWNERS = 32
TOKENS = 131072
IMG_ROWS = 16384
N_DP = 32
N_TENSOR = 16


def draw_positions(key, part):
    key = jax.random.fold_in(key, 11)
    blocks = IMG_ROWS // IMG_DEV
    keys = jax.random.split(key, blocks)

    def one_block(block_key):
        order = jax.random.permutation(block_key, TOK_DEV)
        return jnp.sort(order[:IMG_DEV])
    return jax.vmap(one_block)(keys).reshape(-1).astype(jnp.int32)


def levels(own_key, dims, cuts, low, high):
    factor_of, own = 1.0, jax.random.fold_in(own_key, 6)
    for axis_at, blocks in cuts:
        heights = jnp.exp(jax.random.uniform(jax.random.fold_in(own, axis_at), (blocks,), jnp.float32, low / len(cuts), high / len(cuts)))
        factor_of = factor_of * jnp.repeat(heights, dims[axis_at] // blocks).reshape([-1 if axis == axis_at else 1 for axis in range(len(dims))])
    return factor_of


def assign_block(key, own, number, rows, count, top, most, slope):
    sequence = jax.random.permutation(key, count)
    crowded, common = portions_of(count, rows * top, most, slope, True), portions_of(count, rows * top, most, slope, False)
    places = jnp.arange(count)

    def named(sizes, rotation):
        used = int((sizes > 0).sum())
        fixed = max(1, used // 4)
        shifted = fixed + (places - fixed + rotation * (used - fixed)) % max(1, count - fixed)
        return jnp.zeros((count,), jnp.int32).at[sequence[jnp.where(places < fixed, places, shifted)]].set(jnp.asarray(sizes, jnp.int32))

    sizes = jnp.where(number % 4 == 0, named(crowded, number // 4), named(common, number - number // 4 - 1))
    mixed = jax.random.permutation(jax.random.fold_in(own, 3), count)
    giver, taker = mixed[0:count // 2 * 2:2], mixed[1:count // 2 * 2:2]
    room = jnp.minimum(sizes[giver] - 1, most - sizes[taker]) // 2
    room = jnp.where((giver == sequence[0]) | (taker == sequence[0]) | (sizes[taker] == 0), 0, jnp.maximum(room, 0))
    shifted = jax.random.randint(jax.random.fold_in(own, 4), (count // 2,), 0, 1 << 20) % (room + 1)
    sizes = sizes.at[giver].add(-shifted).at[taker].add(shifted)
    labels = jnp.searchsorted(jnp.cumsum(sizes), jnp.arange(rows * top), side="right").astype(jnp.int32)
    listing = labels.reshape(top, rows).T
    listing = listing[jax.random.permutation(jax.random.fold_in(own, 1), rows)]
    rotation = jax.random.randint(jax.random.fold_in(own, 2), (rows, 1), 0, top)
    return jnp.take_along_axis(listing, (jnp.arange(top)[None, :] + rotation) % top, axis=1)


def portions_of(number_of, total, reach, lean, full):
    weights = [(1 << 20) // math.isqrt(standing ** lean) + 1 for standing in range(1, number_of + 1)]
    largest = reach if full else min(reach, max(-(-total // number_of), total * weights[0] // sum(weights)))
    least = 1 if total - largest >= number_of - 1 else 0
    holding, spare = [largest] + [least] * (number_of - 1), total - largest - least * (number_of - 1)
    while spare > 0:
        candidates = [i for i in range(1, number_of) if holding[i] < largest] or [i for i in range(1, number_of) if holding[i] < reach]
        mass, left = sum([weights[i] for i in candidates]), spare
        for i in candidates:
            addition = min(reach - holding[i], max(1, left * weights[i] // mass), spare)
            holding[i] = holding[i] + addition
            spare = spare - addition
    return np.array(holding)


def bell_draw(stream_key, shape, deviation, most, cuts=(), held_as=jnp.bfloat16):
    factor_of = levels(stream_key, shape, cuts, -0.22, 0.18) if cuts else 1.0
    drawn = jax.random.normal(stream_key, shape, jnp.float32) * deviation * factor_of
    return jnp.minimum(jnp.maximum(drawn, -most), most).astype(held_as)


def setup_inputs(seed: int = 0) -> dict:
    key_of = jax.random.split(jax.random.key(seed), 6)
    grad_hidden = bell_draw(key_of[0], (TOKENS, D), 1.0, 6.0, ((0, 512),))
    positions = draw_positions(jax.random.fold_in(key_of[5], 71), 0)
    owner_ids_keys = jax.random.split(jax.random.fold_in(key_of[2], 1), IMG_ROWS // IMG_DEV)
    owner_ids_turns = jax.random.permutation(jax.random.fold_in(key_of[2], 3), IMG_ROWS // IMG_DEV)
    owner_ids = jax.vmap(lambda own, number: assign_block(jax.random.fold_in(key_of[2], 2), own, number, IMG_DEV, N_DP, 1, CAP, 2))(owner_ids_keys, owner_ids_turns).reshape((IMG_ROWS, 1))
    w_proj = bell_draw(key_of[3], (HID, D), D ** -0.5, 0.09375, ((0, 16), (1, 32)))
    pre_act = bell_draw(key_of[4], (OWNERS, SLOTS, HID), 1.0, 5.0, ((0, 32), (2, 16)))
    return {"grad_hidden": grad_hidden, "positions": positions, "owner_ids": owner_ids, "w_proj": w_proj, "pre_act": pre_act}


def gelu_slope(value):
    return 0.5 * (1.0 + jax.scipy.special.erf(value * 0.7071067811865476)) + value * jnp.exp(-0.5 * value * value) * 0.3989422804014327


def reference(grad_hidden, positions, owner_ids, w_proj, pre_act):
    blocks = N_DP * N_TENSOR
    tokens = grad_hidden.reshape(blocks, TOK_DEV, D)
    where = positions.reshape(blocks, IMG_DEV).astype(jnp.int32)
    image_rows = jnp.take_along_axis(tokens, where[:, :, None], axis=1).reshape(blocks * IMG_DEV, D)
    owners = owner_ids.reshape(blocks, IMG_DEV).astype(jnp.int32)
    onehot = (owners[:, :, None] == jnp.arange(N_DP, dtype=jnp.int32)[None, None, :]).astype(jnp.int32)
    before = jnp.cumsum(onehot, axis=1) - onehot
    rank = jnp.sum(before * onehot, axis=2)
    block_ids = jnp.arange(blocks, dtype=jnp.int32)
    base = (N_DP * (block_ids % N_TENSOR) + block_ids // N_TENSOR) * CAP
    slot = (base[:, None] + rank).reshape(-1)
    projected_rows = jnp.dot(image_rows, w_proj.T, preferred_element_type=jnp.float32)
    projected = jnp.zeros((N_DP, SLOTS, HID), jnp.float32)
    projected = projected.at[owners.reshape(-1), slot].set(projected_rows)
    values = pre_act.astype(jnp.float32)
    return (gelu_slope(values) * projected).astype(jnp.bfloat16)
```

```python
import jax
import jax.numpy as jnp
import numpy as np
from jax import lax
from jax.experimental import pallas as pl
from jax.experimental.pallas import tpu as pltpu
from jax.sharding import Mesh, PartitionSpec as P

AXES = ("x", "zhi", "y", "zlo", "core")
SIZES = (4, 2, 4, 8, 2)
RING = ("zhi", "zlo")
PLANE = ("x", "y")
CODE_LANES = 128
GROUPS = ((0, -1, 1, -2), (2, -3, 3, -4), (4, -5, 5, -6), (6, -7, 7, 8))


def gelu_slope(value):
    return (
        0.5 * (1.0 + jax.scipy.special.erf(value * 0.7071067811865476))
        + value * jnp.exp(-0.5 * value * value) * 0.3989422804014327
    )


def slot_numbers(owner_ids, owner_count, cap_size):
    owners = owner_ids[:, 0]
    onehot = (owners[:, None] == jnp.arange(owner_count, dtype=jnp.int32)[None, :]).astype(
        jnp.int32
    )
    before = jnp.cumsum(onehot, axis=0) - onehot
    rank = jnp.sum(before * onehot, axis=1)
    return owners * cap_size + rank


def dispatch_kernel(zhi_ref, *refs):
    chunks, out_ref = refs[:-1], refs[-1]
    count = len(chunks)
    total, width = out_ref.shape
    rows = chunks[0].shape[0]
    target = lax.broadcasted_iota(jnp.int32, (rows, total), 1)
    rank = target % 2
    member = (target // 2) % count
    plane = target // (2 * count)
    wanted = (((plane // 4) * 8 + zhi_ref[0] * 4 + plane % 4) * 2 + rank).astype(jnp.float32)
    acc = None
    for at, chunk in enumerate(chunks):
        code = chunk[:, width : width + 1].astype(jnp.float32)
        pick = jnp.where((code == wanted) & (member == at), 1.0, 0.0).astype(jnp.bfloat16)
        part = lax.dot_general(
            pick,
            chunk[:, :width],
            (((0,), (0,)), ((), ())),
            preferred_element_type=jnp.float32,
        )
        acc = part if acc is None else acc + part
    out_ref[...] = acc.astype(out_ref.dtype)


def dispatch(chunks, zhi, width):
    total = 32 * len(chunks)
    return pl.pallas_call(
        dispatch_kernel,
        out_shape=jax.ShapeDtypeStruct((total, width), jnp.bfloat16),
        in_specs=[pl.BlockSpec(memory_space=pltpu.SMEM)]
        + [pl.BlockSpec(memory_space=pltpu.VMEM)] * len(chunks),
        out_specs=pl.BlockSpec(memory_space=pltpu.VMEM),
        compiler_params=pltpu.CompilerParams(vmem_limit_bytes=24 * 1024 * 1024),
        cost_estimate=pl.CostEstimate(
            flops=2 * 32 * total * width * len(chunks),
            bytes_accessed=4 * total * width,
            transcendentals=0,
        ),
    )(zhi, *chunks)


def shift(n, step):
    return [(i, (i + step) % n) for i in range(n)]


def final_slots(z, core):
    pieces = []
    for from_core in (core, 1 - core):
        for group in GROUPS:
            offset = jnp.asarray(np.array(group, np.int32))
            source = (z + offset + 16) % 16
            lead = ((source % 8) * 2 + from_core) * 32 + (source // 8) * 4
            plane = np.arange(16)
            plane = jnp.asarray(((plane // 4) * 8 + plane % 4).astype(np.int32))
            slot = (lead[None, :, None] + plane[:, None, None]) * 2 + jnp.arange(2, dtype=jnp.int32)
            pieces.append(slot.reshape(-1))
    return jnp.concatenate(pieces)


def shards(grad_hidden, positions, owner_ids, w_proj, pre_act):
    zhi, zlo, core = (lax.axis_index(name) for name in ("zhi", "zlo", "core"))
    z = zhi * 8 + zlo
    width = grad_hidden.shape[1]
    hidden = w_proj.shape[0]
    zhi_at = jnp.reshape(zhi, (1,)).astype(jnp.int32)

    rows = jnp.take(grad_hidden, positions, axis=0)
    code = slot_numbers(owner_ids, 32, 2).astype(jnp.bfloat16)
    packed = jnp.concatenate(
        [rows, jnp.broadcast_to(code[:, None], (code.shape[0], CODE_LANES))], axis=1
    )

    other = lax.ppermute(w_proj, "zhi", shift(2, 1))
    both = jnp.where(zhi == 0, jnp.stack([w_proj, other]), jnp.stack([other, w_proj]))
    weights = lax.all_gather(both, PLANE, axis=0, tiled=False)
    weights = weights.reshape(4, 4, 2, hidden, 128).transpose(3, 0, 2, 1, 4).reshape(hidden, width)

    held = {0: packed}
    for step in range(1, 8):
        held[-step] = lax.ppermute(held[1 - step], RING, shift(16, 1))
        held[step] = lax.ppermute(held[step - 1], RING, shift(16, 15))
    half = packed.shape[0] // 2
    held[8] = jnp.concatenate(
        [
            lax.ppermute(held[-7][:half], RING, shift(16, 1)),
            lax.ppermute(held[7][half:], RING, shift(16, 15)),
        ]
    )

    own, peer = [], []
    for group in GROUPS:
        count = len(group)
        outgoing = dispatch([held[offset] for offset in group], zhi_at, width)
        received = lax.all_to_all(
            outgoing.reshape(16, 2 * count, width), PLANE, split_axis=0, concat_axis=0, tiled=True
        ).reshape(32 * count, width)
        own.append(received)
        peer.append(lax.ppermute(received, "core", shift(2, 1)))

    contract = (((1,), (1,)), ((), ()))
    projected = [
        lax.dot_general(weights, part, contract, preferred_element_type=jnp.float32)
        for part in own + peer
    ]
    projected = jnp.concatenate(projected, axis=1)

    slots = final_slots(z, core)
    place = (slots[:, None] == jnp.arange(1024, dtype=jnp.int32)[None, :]).astype(jnp.bfloat16)
    values = lax.dot_general(
        pre_act[0].T, place, contract, preferred_element_type=jnp.float32
    )
    gradient = (gelu_slope(values) * projected).astype(jnp.bfloat16)
    placed = jnp.dot(gradient, place, preferred_element_type=jnp.float32).astype(jnp.bfloat16)
    return placed.T[None]


def solution(mesh):
    fine = Mesh(mesh.devices.reshape(SIZES), AXES)
    return jax.shard_map(
        shards,
        mesh=fine,
        in_specs=(
            P(AXES, None),
            P(AXES),
            P(AXES, None),
            P(("zlo", "core"), ("x", "zhi", "y")),
            P(("x", "zhi", "y"), None, ("zlo", "core")),
        ),
        out_specs=P(("x", "zhi", "y"), None, ("zlo", "core")),
        check_vma=False,
    )
```

```python
import jax
import jax.numpy as jnp
from jax import lax
from jax.experimental import pallas as pl
from jax.experimental.pallas import tpu as pltpu
from jax.sharding import Mesh, PartitionSpec as P

AXES = ("x", "zhi", "y", "zlo", "core")
SIZES = (4, 2, 4, 8, 2)
RING = ("zhi", "zlo", "core")
PLANE = ("x", "y")
CODE_LANES = 128
IMG = 32
SLOTS = 1024
STEPS = 8
NT = (((1,), (1,)), ((), ()))
TN = (((0,), (0,)), ((), ()))
VMEM = pl.BlockSpec(memory_space=pltpu.VMEM)
SMEM = pl.BlockSpec(memory_space=pltpu.SMEM)


def gelu_slope(value):
    return (
        0.5 * (1.0 + lax.erf(value * 0.7071067811865476))
        + value * jnp.exp(-0.5 * value * value) * 0.3989422804014327
    )


def params(mib):
    return pltpu.CompilerParams(vmem_limit_bytes=mib * 1024 * 1024)


def pick_kernel(positions_ref, owners_ref, hidden_ref, out_ref):
    step = pl.program_id(0)
    row = lax.broadcasted_iota(jnp.int32, (IMG, IMG), 0)
    lane = lax.broadcasted_iota(jnp.int32, (IMG, IMG), 1)

    def column(ref):
        spread = jnp.broadcast_to(ref[...], (IMG, IMG))
        return spread, jnp.sum(jnp.where(row == lane, spread, 0), axis=1, keepdims=True)

    _, at = column(positions_ref)
    token = lax.broadcasted_iota(jnp.int32, (IMG, hidden_ref.shape[0]), 1)
    pick = jnp.where(token == at, 1.0, 0.0).astype(jnp.bfloat16)
    picked = jnp.dot(pick, hidden_ref[...], preferred_element_type=jnp.float32).astype(
        jnp.bfloat16
    )
    x, zhi = step // 2, step % 2
    for y in range(4):
        start = pl.multiple_of((x * 8 + y * 2 + zhi) * 128, 128)
        out_ref[:, pl.ds(start, 128)] = picked[:, y * 128 : (y + 1) * 128]

    @pl.when(step == 0)
    def _():
        spread, owner = column(owners_ref)
        same = jnp.where((spread == owner) & (lane < row), 1, 0)
        code = owner * 2 + jnp.sum(same, axis=1, keepdims=True)
        width = out_ref.shape[1] - CODE_LANES
        out_ref[:, width:] = jnp.broadcast_to(
            code.astype(jnp.float32), (IMG, CODE_LANES)
        ).astype(jnp.bfloat16)


def pick(grad_hidden, positions, owner_ids):
    tokens, width = grad_hidden.shape
    return pl.pallas_call(
        pick_kernel,
        grid=(8,),
        out_shape=jax.ShapeDtypeStruct((IMG, width + CODE_LANES), jnp.bfloat16),
        in_specs=[
            pl.BlockSpec((1, IMG), lambda i: (0, 0)),
            pl.BlockSpec((1, IMG), lambda i: (0, 0)),
            pl.BlockSpec((tokens, width // 8), lambda i: (0, i)),
        ],
        out_specs=pl.BlockSpec((IMG, width + CODE_LANES), lambda i: (0, 0)),
        compiler_params=params(8),
        cost_estimate=pl.CostEstimate(
            flops=2 * IMG * tokens * width, bytes_accessed=2 * tokens * width, transcendentals=0
        ),
    )(positions.reshape(1, IMG), owner_ids.reshape(1, IMG), grad_hidden)


def dispatch_kernel(zhi_ref, *refs):
    chunks, out_ref = refs[:-1], refs[-1]
    count = len(chunks)
    total, width = out_ref.shape
    target = lax.broadcasted_iota(jnp.int32, (IMG, total), 1)
    rank = target % 2
    member = (target // 2) % count
    plane = target // (2 * count)
    wanted = (((plane // 4) * 8 + zhi_ref[0] * 4 + plane % 4) * 2 + rank).astype(jnp.float32)
    picks = []
    for at, chunk in enumerate(chunks):
        code = chunk[:, width : width + 1].astype(jnp.float32)
        chosen = jnp.where((code == wanted) & (member == at), 1.0, 0.0)
        picks.append(chosen.astype(jnp.bfloat16))
    for start in range(0, width, 512):
        acc = None
        for chosen, chunk in zip(picks, chunks):
            part = lax.dot_general(
                chosen, chunk[:, start : start + 512], TN, preferred_element_type=jnp.float32
            )
            acc = part if acc is None else acc + part
        out_ref[:, start : start + 512] = acc.astype(out_ref.dtype)


def dispatch(chunks, zhi, width):
    total = IMG * len(chunks)
    return pl.pallas_call(
        dispatch_kernel,
        out_shape=jax.ShapeDtypeStruct((total, width), jnp.bfloat16),
        in_specs=[SMEM] + [VMEM] * len(chunks),
        out_specs=VMEM,
        compiler_params=params(8),
        cost_estimate=pl.CostEstimate(
            flops=2 * IMG * total * width * len(chunks),
            bytes_accessed=4 * total * width,
            transcendentals=0,
        ),
    )(zhi, *chunks)


def slope_kernel(place_ref, pre_ref, slope_ref, place_out):
    z, core = place_ref[0], place_ref[1]
    at = lax.broadcasted_iota(jnp.int32, (SLOTS, 1), 0)
    rank = at & 1
    chunk = ((at >> 7) & 3) * 4 + ((at >> 1) & 3)
    y = (at >> 3) & 3
    x = (at >> 5) & 3
    gatherer = jnp.where(at >= SLOTS // 2, 1 - core, core)
    distance = (chunk + 1) >> 1
    source = (z + 16 + jnp.where(gatherer == 0, -distance, distance)) & 15
    kept = (chunk == 0) | ((chunk & 1) == 1)
    from_core = jnp.where(kept, gatherer, 1 - gatherer)
    tensor = (source & 7) * 2 + from_core
    slot = (tensor * 32 + x * 8 + (source >> 3) * 4 + y) * 2 + rank
    final = lax.broadcasted_iota(jnp.int32, (SLOTS, SLOTS), 1)
    place = jnp.where(slot == final, 1.0, 0.0).astype(jnp.bfloat16)
    place_out[...] = place
    values = lax.dot_general(pre_ref[...], place, NT, preferred_element_type=jnp.float32)
    slope_ref[...] = gelu_slope(values)


def slopes(z, core, pre):
    return pl.pallas_call(
        slope_kernel,
        out_shape=(
            jax.ShapeDtypeStruct(pre.shape, jnp.float32),
            jax.ShapeDtypeStruct((SLOTS, SLOTS), jnp.bfloat16),
        ),
        in_specs=[SMEM, VMEM],
        out_specs=(VMEM, VMEM),
        compiler_params=params(24),
        cost_estimate=pl.CostEstimate(
            flops=2 * pre.shape[0] * SLOTS * SLOTS,
            bytes_accessed=4 * SLOTS * SLOTS,
            transcendentals=2 * pre.shape[0] * SLOTS,
        ),
    )(jnp.stack([z, core]).astype(jnp.int32), pre)


def project_kernel(weights_ref, *refs):
    parts, out_ref = refs[:-1], refs[-1]
    start = 0
    for part in parts:
        size = part.shape[0]
        out_ref[:, start : start + size] = lax.dot_general(
            weights_ref[...], part[...], NT, preferred_element_type=jnp.float32
        )
        start += size


def project(weights, parts):
    hidden, width = weights.shape
    total = sum(part.shape[0] for part in parts)
    return pl.pallas_call(
        project_kernel,
        out_shape=jax.ShapeDtypeStruct((hidden, total), jnp.float32),
        in_specs=[VMEM] * (1 + len(parts)),
        out_specs=VMEM,
        compiler_params=params(24),
        cost_estimate=pl.CostEstimate(
            flops=2 * hidden * width * total, bytes_accessed=2 * width * total, transcendentals=0
        ),
    )(weights, *parts)


def finish_kernel(weights_ref, part_ref, early_ref, slope_ref, place_ref, out_ref):
    early = early_ref.shape[1]
    last = lax.dot_general(
        weights_ref[...], part_ref[...], NT, preferred_element_type=jnp.float32
    )
    first = (slope_ref[:, :early] * early_ref[...]).astype(jnp.bfloat16)
    last = (slope_ref[:, early:] * last).astype(jnp.bfloat16)
    placed = jnp.dot(first, place_ref[:early], preferred_element_type=jnp.float32)
    placed += jnp.dot(last, place_ref[early:], preferred_element_type=jnp.float32)
    out_ref[...] = placed.astype(out_ref.dtype)


def finish(weights, part, early, slope, place):
    hidden, width = weights.shape
    return pl.pallas_call(
        finish_kernel,
        out_shape=jax.ShapeDtypeStruct((hidden, SLOTS), jnp.bfloat16),
        in_specs=[VMEM] * 5,
        out_specs=VMEM,
        compiler_params=params(24),
        cost_estimate=pl.CostEstimate(
            flops=2 * hidden * (width * part.shape[0] + SLOTS * SLOTS),
            bytes_accessed=2 * SLOTS * SLOTS,
            transcendentals=0,
        ),
    )(weights, part, early, slope, place)


def ring_pairs(other_core):
    pairs = []
    for z in range(16):
        for core in range(2):
            below = (z + (-1 if core == 0 else 1)) % 16
            sender = 1 - core if other_core else core
            pairs.append((below * 2 + sender, z * 2 + core))
    return pairs


def shards(grad_hidden, positions, owner_ids, w_proj, pre_act):
    zhi, zlo, core = (lax.axis_index(name) for name in ("zhi", "zlo", "core"))
    width = grad_hidden.shape[1]
    zhi_at = jnp.reshape(zhi, (1,)).astype(jnp.int32)
    swap = [(0, 1), (1, 0)]

    packed = pick(grad_hidden, positions, owner_ids)

    kept, crossed = [packed], [packed]
    for step in range(1, STEPS + 1):
        kept.append(lax.ppermute(kept[-1], RING, ring_pairs(False)))
        if step < STEPS:
            crossed.append(lax.ppermute(crossed[-1], RING, ring_pairs(step == 1)))
    chunks = [packed]
    for step in range(1, STEPS + 1):
        chunks.append(kept[step])
        if step < STEPS:
            chunks.append(crossed[step])

    other = lax.ppermute(w_proj, "zhi", swap)
    both = jnp.concatenate(
        [jnp.where(zhi == 0, w_proj, other), jnp.where(zhi == 0, other, w_proj)], axis=1
    )
    weights = lax.all_gather(both, PLANE, axis=1, tiled=True)

    slope, place = slopes(zhi * 8 + zlo, core, pre_act[0].T)

    own, peer = [], []
    for group in range(4):
        if group == 2:
            zhi_at, slope, place = lax.optimization_barrier((zhi_at, slope, place))
        outgoing = dispatch(chunks[4 * group : 4 * group + 4], zhi_at, width)
        received = lax.all_to_all(
            outgoing.reshape(16, 8, width), PLANE, split_axis=0, concat_axis=0, tiled=True
        ).reshape(4 * IMG, width)
        own.append(received)
        peer.append(lax.ppermute(received, "core", swap))

    early = project(weights, own + peer[:3])
    gradient = finish(weights, peer[3], early, slope, place)
    return gradient.T[None]


def solution(mesh):
    fine = Mesh(mesh.devices.reshape(SIZES), AXES)
    return jax.shard_map(
        shards,
        mesh=fine,
        in_specs=(
            P(AXES, None),
            P(AXES),
            P(AXES, None),
            P(("zlo", "core"), ("x", "zhi", "y")),
            P(("x", "zhi", "y"), None, ("zlo", "core")),
        ),
        out_specs=P(("x", "zhi", "y"), None, ("zlo", "core")),
        check_vma=False,
    )
```

```python
import functools

import jax
import jax.numpy as jnp
import numpy as np
from jax import lax
from jax.experimental import pallas as pl
from jax.experimental.pallas import tpu as pltpu
from jax.sharding import Mesh, PartitionSpec as P

AXES = ("x", "zhi", "y", "zlo", "core")
SIZES = (4, 2, 4, 8, 2)
RING = ("zhi", "zlo", "core")
PLANE = ("x", "y")
CODE_LANES = 128
TILE = 256
IMG = 32
SLOTS = 1024
MINE = SLOTS // 2
STEPS = 8
GROUPS = (8, 8)
WEIGHTS_BY = 2
NT = (((1,), (1,)), ((), ()))
TN = (((0,), (0,)), ((), ()))
VMEM = pl.BlockSpec(memory_space=pltpu.VMEM)
SMEM = pl.BlockSpec(memory_space=pltpu.SMEM)


def gelu_slope(value):
    return (
        0.5 * (1.0 + lax.erf(value * 0.7071067811865476))
        + value * jnp.exp(-0.5 * value * value) * 0.3989422804014327
    )


def params(mib):
    return pltpu.CompilerParams(vmem_limit_bytes=mib * 1024 * 1024)


def pick_kernel(positions_hbm, owners_hbm, hidden_hbm, out_ref, positions, owners, hidden, sems):
    tiles = hidden.shape[0]
    tile = hidden.shape[2]
    copies = [
        pltpu.make_async_copy(positions_hbm, positions, sems.at[tiles]),
        pltpu.make_async_copy(owners_hbm, owners, sems.at[tiles + 1]),
    ]
    for at in range(tiles):
        source = hidden_hbm.at[:, at * tile : (at + 1) * tile]
        copies.append(pltpu.make_async_copy(source, hidden.at[at], sems.at[at]))
    for copy in copies:
        copy.start()
    row = lax.broadcasted_iota(jnp.int32, (IMG, IMG), 0)
    lane = lax.broadcasted_iota(jnp.int32, (IMG, IMG), 1)

    def column(ref):
        spread = jnp.broadcast_to(ref[...], (IMG, IMG))
        return spread, jnp.sum(jnp.where(row == lane, spread, 0), axis=1, keepdims=True)

    copies[0].wait()
    _, place = column(positions)
    token = lax.broadcasted_iota(jnp.int32, (IMG, hidden.shape[1]), 1)
    pick = jnp.where(token == place, 1.0, 0.0).astype(jnp.bfloat16)
    copies[1].wait()
    spread, owner = column(owners)
    same = jnp.where((spread == owner) & (lane < row), 1, 0)
    code = owner * 2 + jnp.sum(same, axis=1, keepdims=True)
    width = out_ref.shape[1] - CODE_LANES
    out_ref[:, width:] = jnp.broadcast_to(code.astype(jnp.float32), (IMG, CODE_LANES)).astype(
        jnp.bfloat16
    )
    for at in range(tiles):
        copies[2 + at].wait()
        picked = jnp.dot(pick, hidden[at], preferred_element_type=jnp.float32)
        picked = picked.astype(jnp.bfloat16)
        x, zhi = at // 2, at % 2
        for y in range(4):
            start = (x * 8 + y * 2 + zhi) * 128
            out_ref[:, start : start + 128] = picked[:, y * 128 : (y + 1) * 128]


def pick(grad_hidden, positions, owner_ids):
    tokens, width = grad_hidden.shape
    tiles = 8
    return pl.pallas_call(
        pick_kernel,
        out_shape=jax.ShapeDtypeStruct((IMG, width + CODE_LANES), jnp.bfloat16),
        in_specs=[pl.BlockSpec(memory_space=pltpu.HBM)] * 3,
        out_specs=VMEM,
        scratch_shapes=[
            pltpu.VMEM((1, IMG), jnp.int32),
            pltpu.VMEM((1, IMG), jnp.int32),
            pltpu.VMEM((tiles, tokens, width // tiles), jnp.bfloat16),
            pltpu.SemaphoreType.DMA((tiles + 2,)),
        ],
        compiler_params=params(60),
        cost_estimate=pl.CostEstimate(
            flops=2 * IMG * tokens * width, bytes_accessed=2 * tokens * width, transcendentals=0
        ),
    )(positions.reshape(1, IMG), owner_ids.reshape(1, IMG), grad_hidden)


def dispatch_kernel(zhi_ref, *refs):
    chunks, out_ref = refs[:-1], refs[-1]
    width = chunks[0].shape[1] - CODE_LANES
    height = 2 * len(chunks)
    size = 4 * IMG
    target = lax.broadcasted_iota(jnp.int32, (IMG, size), 1)
    rank = target & 1
    member = (target >> 1) & 3
    plane = target >> 3
    wanted = (((plane >> 2) * 8 + zhi_ref[0] * 4 + (plane & 3)) * 2 + rank).astype(jnp.float32)
    for first in range(0, len(chunks), 4):
        group = chunks[first : first + 4]
        picks = []
        for at, chunk in enumerate(group):
            code = chunk[:, width : width + 1].astype(jnp.float32)
            picks.append(jnp.where((code == wanted) & (member == at), 1.0, 0.0))
        pick = jnp.concatenate(picks, axis=0).T.astype(jnp.bfloat16)
        for tile in range(width // TILE):
            columns = slice(tile * TILE, (tile + 1) * TILE)
            rows = jnp.concatenate([chunk[:, columns] for chunk in group], axis=0)
            moved = jnp.dot(pick, rows, preferred_element_type=jnp.float32).astype(out_ref.dtype)
            top = tile * height + 2 * first
            out_ref[:, top : top + 8, :] = moved.reshape(16, 8, TILE)


def dispatch(chunks, zhi, width):
    count = len(chunks)
    height = 2 * count * (width // TILE)
    return pl.pallas_call(
        dispatch_kernel,
        out_shape=jax.ShapeDtypeStruct((16, height, TILE), jnp.bfloat16),
        in_specs=[SMEM] + [VMEM] * count,
        out_specs=VMEM,
        compiler_params=params(16),
        cost_estimate=pl.CostEstimate(
            flops=2 * 4 * IMG * IMG * count * width,
            bytes_accessed=2 * 16 * height * TILE,
            transcendentals=0,
        ),
    )(zhi, *chunks)


def arrival_table():
    table = []
    first = 0
    for count in GROUPS:
        for plane in range(16):
            for block in range(first, first + count):
                kept = 1 if block == 0 or block % 2 == 1 else 0
                info = (block + 1) // 2 + 16 * kept + 256 * ((plane // 4) * 8 + plane % 4)
                table += [info, info + 64]
        first += count
    return np.array(table, np.int32).reshape(MINE, 1)


def slope_kernel(at_ref, table_ref, pre_ref, pre_other_ref, slope_ref, here_ref, there_ref):
    z, core = at_ref[0], at_ref[1]
    info = table_ref[...]
    distance = info & 15
    kept = (info >> 4) & 1
    rank = (info >> 6) & 1
    plane = info >> 8
    final = lax.broadcasted_iota(jnp.int32, (MINE, SLOTS), 1)

    def places(gatherer):
        source = (z + 16 + jnp.where(gatherer == 0, -distance, distance)) & 15
        from_core = jnp.where(kept == 1, gatherer, 1 - gatherer)
        tensor = (source & 7) * 2 + from_core
        slot = (tensor * 32 + plane + (source >> 3) * 4) * 2 + rank
        return jnp.where(slot == final, 1.0, 0.0).astype(jnp.bfloat16)

    here = places(core)
    here_ref[...] = here
    there_ref[...] = places(1 - core)
    hidden = pre_ref.shape[0]
    for start, ref in ((0, pre_ref), (hidden, pre_other_ref)):
        values = lax.dot_general(ref[...], here, NT, preferred_element_type=jnp.float32)
        slope_ref[start : start + hidden, :] = gelu_slope(values)


def slopes(z, core, pre, pre_other):
    hidden = pre.shape[0]
    place = jax.ShapeDtypeStruct((MINE, SLOTS), jnp.bfloat16)
    return pl.pallas_call(
        slope_kernel,
        out_shape=(jax.ShapeDtypeStruct((2 * hidden, MINE), jnp.float32), place, place),
        in_specs=[SMEM, VMEM, VMEM, VMEM],
        out_specs=(VMEM, VMEM, VMEM),
        compiler_params=params(16),
        cost_estimate=pl.CostEstimate(
            flops=4 * hidden * MINE * SLOTS,
            bytes_accessed=4 * SLOTS * SLOTS,
            transcendentals=4 * hidden * MINE,
        ),
    )(jnp.stack([z, core]).astype(jnp.int32), jnp.asarray(arrival_table()), pre, pre_other)


def project_kernel(first, core_ref, weights_ref, slope_ref, rows_ref, here_ref, there_ref):
    hidden, count = here_ref.shape
    tiles = weights_ref.shape[0] // 2
    mine, other = core_ref[0] * tiles, (1 - core_ref[0]) * tiles
    height = count // 16
    projected = None
    for tile in range(tiles):
        rows = rows_ref[:, tile * height : (tile + 1) * height, :].reshape(count, TILE)
        weights = jnp.concatenate([weights_ref[mine + tile], weights_ref[other + tile]], axis=0)
        part = lax.dot_general(weights, rows, NT, preferred_element_type=jnp.float32)
        projected = part if projected is None else projected + part
    gradient = (slope_ref[:, first : first + count] * projected).astype(jnp.bfloat16)
    here_ref[...] = gradient[:hidden]
    there_ref[...] = gradient[hidden:]


def project(core, weights, slope, rows, first, count):
    tiles, hidden, _ = weights.shape
    half = jax.ShapeDtypeStruct((hidden, count), jnp.bfloat16)
    return pl.pallas_call(
        functools.partial(project_kernel, first),
        out_shape=(half, half),
        in_specs=[SMEM] + [VMEM] * 3,
        out_specs=(VMEM, VMEM),
        compiler_params=params(24),
        cost_estimate=pl.CostEstimate(
            flops=2 * hidden * tiles * TILE * count,
            bytes_accessed=2 * weights.size,
            transcendentals=0,
        ),
    )(core, weights, slope, rows)


def place_kernel(first, *refs):
    here_ref, there_ref, here_place_ref, there_place_ref = refs[-5:-1]
    out_ref = refs[-1]
    span = slice(first, first + here_ref.shape[1])
    placed = jnp.dot(here_ref[...], here_place_ref[span, :], preferred_element_type=jnp.float32)
    placed += jnp.dot(there_ref[...], there_place_ref[span, :], preferred_element_type=jnp.float32)
    if len(refs) > 5:
        placed += refs[0][...].astype(jnp.float32)
    out_ref[...] = placed.astype(out_ref.dtype)


def put(here, there, here_place, there_place, first, base):
    hidden = here.shape[0]
    operands = base + [here, there, here_place, there_place]
    return pl.pallas_call(
        functools.partial(place_kernel, first),
        out_shape=jax.ShapeDtypeStruct((hidden, SLOTS), jnp.bfloat16),
        in_specs=[VMEM] * len(operands),
        out_specs=VMEM,
        compiler_params=params(16),
        cost_estimate=pl.CostEstimate(
            flops=4 * hidden * here.shape[1] * SLOTS,
            bytes_accessed=4 * SLOTS * here.shape[1],
            transcendentals=0,
        ),
    )(*operands)


def ring_pairs(other_core):
    pairs = []
    for z in range(16):
        for core in range(2):
            below = (z + (-1 if core == 0 else 1)) % 16
            sender = 1 - core if other_core else core
            pairs.append((below * 2 + sender, z * 2 + core))
    return pairs


def shards(grad_hidden, positions, owner_ids, w_proj, pre_act):
    zhi, zlo, core = (lax.axis_index(name) for name in ("zhi", "zlo", "core"))
    width = grad_hidden.shape[1]
    zhi_at = jnp.reshape(zhi, (1,)).astype(jnp.int32)
    core_at = jnp.reshape(core, (1,)).astype(jnp.int32)
    swap = [(0, 1), (1, 0)]

    packed = pick(grad_hidden, positions, owner_ids)

    other = lax.ppermute(w_proj, "zhi", swap)
    both = jnp.concatenate(
        [jnp.where(zhi == 0, w_proj, other), jnp.where(zhi == 0, other, w_proj)], axis=1
    )

    kept, crossed = [packed], [packed]
    for step in range(1, STEPS + 1):
        kept.append(lax.ppermute(kept[-1], RING, ring_pairs(False)))
        if step < STEPS:
            crossed.append(lax.ppermute(crossed[-1], RING, ring_pairs(step == 1)))
        if step == WEIGHTS_BY:
            kept[-1], crossed[-1], both = lax.optimization_barrier((kept[-1], crossed[-1], both))
            weights = lax.all_gather(both, ("core",) + PLANE, axis=0, tiled=False)
    chunks = [packed]
    for step in range(1, STEPS + 1):
        chunks.append(kept[step])
        if step < STEPS:
            chunks.append(crossed[step])

    pre = pre_act[0].T
    slope, here_place, there_place = slopes(
        zhi * 8 + zlo, core, pre, lax.ppermute(pre, "core", swap)
    )

    placed = []
    first = 0
    for count in GROUPS:
        outgoing = dispatch(chunks[first : first + count], zhi_at, width)
        received = lax.all_to_all(outgoing, PLANE, split_axis=0, concat_axis=0, tiled=True)
        here, there = project(core_at, weights, slope, received, first * IMG, count * IMG)
        there = lax.ppermute(there, "core", swap)
        placed = [put(here, there, here_place, there_place, first * IMG, placed)]
        first += count
    return placed[0].T[None]


def solution(mesh):
    fine = Mesh(mesh.devices.reshape(SIZES), AXES)
    return jax.shard_map(
        shards,
        mesh=fine,
        in_specs=(
            P(AXES, None),
            P(AXES),
            P(AXES, None),
            P(("zlo", "core"), ("x", "zhi", "y")),
            P(("x", "zhi", "y"), None, ("zlo", "core")),
        ),
        out_specs=P(("x", "zhi", "y"), None, ("zlo", "core")),
        check_vma=False,
    )
```

```python
import functools

import jax
import jax.numpy as jnp
import numpy as np
from jax import lax
from jax.experimental import pallas as pl
from jax.experimental.pallas import tpu as pltpu
from jax.sharding import Mesh, PartitionSpec as P

AXES = ("x", "zhi", "y", "zlo", "core")
SIZES = (4, 2, 4, 8, 2)
RING = ("zhi", "zlo", "core")
PLANE = ("x", "y")
CODE_LANES = 128
TILE = 256
IMG = 32
SLOTS = 1024
MINE = SLOTS // 2
STEPS = 8
GROUPS = (8, 8)
WEIGHTS_BY = 2
NT = (((1,), (1,)), ((), ()))
TN = (((0,), (0,)), ((), ()))
VMEM = pl.BlockSpec(memory_space=pltpu.VMEM)
SMEM = pl.BlockSpec(memory_space=pltpu.SMEM)


def gelu_slope(value):
    return (
        0.5 * (1.0 + lax.erf(value * 0.7071067811865476))
        + value * jnp.exp(-0.5 * value * value) * 0.3989422804014327
    )


def params(mib):
    return pltpu.CompilerParams(vmem_limit_bytes=mib * 1024 * 1024)


def pick_kernel(positions_hbm, owners_hbm, hidden_hbm, out_ref, positions, owners, hidden, sems):
    tiles = hidden.shape[0]
    tile = hidden.shape[2]
    copies = [
        pltpu.make_async_copy(positions_hbm, positions, sems.at[tiles]),
        pltpu.make_async_copy(owners_hbm, owners, sems.at[tiles + 1]),
    ]
    for at in range(tiles):
        source = hidden_hbm.at[:, at * tile : (at + 1) * tile]
        copies.append(pltpu.make_async_copy(source, hidden.at[at], sems.at[at]))
    for copy in copies:
        copy.start()
    row = lax.broadcasted_iota(jnp.int32, (IMG, IMG), 0)
    lane = lax.broadcasted_iota(jnp.int32, (IMG, IMG), 1)

    def column(ref):
        spread = jnp.broadcast_to(ref[...], (IMG, IMG))
        return spread, jnp.sum(jnp.where(row == lane, spread, 0), axis=1, keepdims=True)

    copies[0].wait()
    _, place = column(positions)
    token = lax.broadcasted_iota(jnp.int32, (IMG, hidden.shape[1]), 1)
    pick = jnp.where(token == place, 1.0, 0.0).astype(jnp.bfloat16)
    copies[1].wait()
    spread, owner = column(owners)
    same = jnp.where((spread == owner) & (lane < row), 1, 0)
    code = owner * 2 + jnp.sum(same, axis=1, keepdims=True)
    width = out_ref.shape[1] - CODE_LANES
    out_ref[:, width:] = jnp.broadcast_to(code.astype(jnp.float32), (IMG, CODE_LANES)).astype(
        jnp.bfloat16
    )
    for at in range(tiles):
        copies[2 + at].wait()
        picked = jnp.dot(pick, hidden[at], preferred_element_type=jnp.float32)
        picked = picked.astype(jnp.bfloat16)
        x, zhi = at // 2, at % 2
        for y in range(4):
            start = (x * 8 + y * 2 + zhi) * 128
            out_ref[:, start : start + 128] = picked[:, y * 128 : (y + 1) * 128]


def pick(grad_hidden, positions, owner_ids):
    tokens, width = grad_hidden.shape
    tiles = 8
    return pl.pallas_call(
        pick_kernel,
        out_shape=jax.ShapeDtypeStruct((IMG, width + CODE_LANES), jnp.bfloat16),
        in_specs=[pl.BlockSpec(memory_space=pltpu.HBM)] * 3,
        out_specs=VMEM,
        scratch_shapes=[
            pltpu.VMEM((1, IMG), jnp.int32),
            pltpu.VMEM((1, IMG), jnp.int32),
            pltpu.VMEM((tiles, tokens, width // tiles), jnp.bfloat16),
            pltpu.SemaphoreType.DMA((tiles + 2,)),
        ],
        compiler_params=params(60),
        cost_estimate=pl.CostEstimate(
            flops=2 * IMG * tokens * width, bytes_accessed=2 * tokens * width, transcendentals=0
        ),
    )(positions.reshape(1, IMG), owner_ids.reshape(1, IMG), grad_hidden)


def dispatch_kernel(zhi_ref, *refs):
    chunks, out_ref = refs[:-1], refs[-1]
    width = chunks[0].shape[1] - CODE_LANES
    height = 2 * len(chunks)
    size = 4 * IMG
    target = lax.broadcasted_iota(jnp.int32, (IMG, size), 1)
    rank = target & 1
    member = (target >> 1) & 3
    plane = target >> 3
    wanted = (((plane >> 2) * 8 + zhi_ref[0] * 4 + (plane & 3)) * 2 + rank).astype(jnp.float32)
    for first in range(0, len(chunks), 4):
        group = chunks[first : first + 4]
        picks = []
        for at, chunk in enumerate(group):
            code = chunk[:, width : width + 1].astype(jnp.float32)
            picks.append(jnp.where((code == wanted) & (member == at), 1.0, 0.0))
        pick = jnp.concatenate(picks, axis=0).T.astype(jnp.bfloat16)
        for tile in range(width // TILE):
            columns = slice(tile * TILE, (tile + 1) * TILE)
            rows = jnp.concatenate([chunk[:, columns] for chunk in group], axis=0)
            moved = jnp.dot(pick, rows, preferred_element_type=jnp.float32).astype(out_ref.dtype)
            top = tile * height + 2 * first
            out_ref[:, top : top + 8, :] = moved.reshape(16, 8, TILE)


def dispatch(chunks, zhi, width):
    count = len(chunks)
    height = 2 * count * (width // TILE)
    return pl.pallas_call(
        dispatch_kernel,
        out_shape=jax.ShapeDtypeStruct((16, height, TILE), jnp.bfloat16),
        in_specs=[SMEM] + [VMEM] * count,
        out_specs=VMEM,
        compiler_params=params(16),
        cost_estimate=pl.CostEstimate(
            flops=2 * 4 * IMG * IMG * count * width,
            bytes_accessed=2 * 16 * height * TILE,
            transcendentals=0,
        ),
    )(zhi, *chunks)


def arrival_table():
    table = []
    first = 0
    for count in GROUPS:
        for plane in range(16):
            for block in range(first, first + count):
                kept = 1 if block == 0 or block % 2 == 1 else 0
                info = (block + 1) // 2 + 16 * kept + 256 * ((plane // 4) * 8 + plane % 4)
                table += [info, info + 64]
        first += count
    return np.array(table, np.int32).reshape(MINE, 1)


def slope_kernel(at_ref, table_ref, pre_ref, pre_other_ref, slope_ref, here_ref, there_ref):
    z, core = at_ref[0], at_ref[1]
    info = table_ref[...]
    distance = info & 15
    kept = (info >> 4) & 1
    rank = (info >> 6) & 1
    plane = info >> 8
    final = lax.broadcasted_iota(jnp.int32, (MINE, SLOTS), 1)

    def places(gatherer):
        source = (z + 16 + jnp.where(gatherer == 0, -distance, distance)) & 15
        from_core = jnp.where(kept == 1, gatherer, 1 - gatherer)
        tensor = (source & 7) * 2 + from_core
        slot = (tensor * 32 + plane + (source >> 3) * 4) * 2 + rank
        return jnp.where(slot == final, 1.0, 0.0).astype(jnp.bfloat16)

    here = places(core)
    here_ref[...] = here
    there_ref[...] = places(1 - core)
    hidden = pre_ref.shape[0]
    for start, ref in ((0, pre_ref), (hidden, pre_other_ref)):
        values = lax.dot_general(ref[...], here, NT, preferred_element_type=jnp.float32)
        slope_ref[start : start + hidden, :] = gelu_slope(values)


def slopes(z, core, pre, pre_other):
    hidden = pre.shape[0]
    place = jax.ShapeDtypeStruct((MINE, SLOTS), jnp.bfloat16)
    return pl.pallas_call(
        slope_kernel,
        out_shape=(jax.ShapeDtypeStruct((2 * hidden, MINE), jnp.float32), place, place),
        in_specs=[SMEM, VMEM, VMEM, VMEM],
        out_specs=(VMEM, VMEM, VMEM),
        compiler_params=params(16),
        cost_estimate=pl.CostEstimate(
            flops=4 * hidden * MINE * SLOTS,
            bytes_accessed=4 * SLOTS * SLOTS,
            transcendentals=4 * hidden * MINE,
        ),
    )(jnp.stack([z, core]).astype(jnp.int32), jnp.asarray(arrival_table()), pre, pre_other)


def project_kernel(first, core_ref, weights_ref, slope_ref, rows_ref, here_ref, there_ref):
    hidden, count = here_ref.shape
    tiles = weights_ref.shape[0] // 2
    mine, other = core_ref[0] * tiles, (1 - core_ref[0]) * tiles
    height = count // 16
    projected = None
    for tile in range(tiles):
        rows = rows_ref[:, tile * height : (tile + 1) * height, :].reshape(count, TILE)
        weights = jnp.concatenate([weights_ref[mine + tile], weights_ref[other + tile]], axis=0)
        part = lax.dot_general(weights, rows, NT, preferred_element_type=jnp.float32)
        projected = part if projected is None else projected + part
    gradient = (slope_ref[:, first : first + count] * projected).astype(jnp.bfloat16)
    here_ref[...] = gradient[:hidden]
    there_ref[...] = gradient[hidden:]


def project(core, weights, slope, rows, first, count):
    tiles, hidden, _ = weights.shape
    half = jax.ShapeDtypeStruct((hidden, count), jnp.bfloat16)
    return pl.pallas_call(
        functools.partial(project_kernel, first),
        out_shape=(half, half),
        in_specs=[SMEM] + [VMEM] * 3,
        out_specs=(VMEM, VMEM),
        compiler_params=params(24),
        cost_estimate=pl.CostEstimate(
            flops=2 * hidden * tiles * TILE * count,
            bytes_accessed=2 * weights.size,
            transcendentals=0,
        ),
    )(core, weights, slope, rows)


def half_kernel(core_ref, weights_ref, slope_ref, rows_ref, out_ref):
    count = out_ref.shape[1]
    height = count // 16
    projected = None
    for tile in range(weights_ref.shape[0]):
        rows = rows_ref[:, tile * height : (tile + 1) * height, :].reshape(count, TILE)
        part = lax.dot_general(weights_ref[tile], rows, NT, preferred_element_type=jnp.float32)
        projected = part if projected is None else projected + part
    out_ref[...] = (slope_ref[...] * projected).astype(jnp.bfloat16)


def project_half(core, weights, slope, rows, first, count, other):
    planes, hidden, _ = weights.shape

    def half_of(i, core):
        return ((1 - core[0]) if other else core[0], 0, 0)

    return pl.pallas_call(
        half_kernel,
        out_shape=jax.ShapeDtypeStruct((hidden, count), jnp.bfloat16),
        grid_spec=pltpu.PrefetchScalarGridSpec(
            num_scalar_prefetch=1,
            grid=(1,),
            in_specs=[
                pl.BlockSpec((planes // 2, hidden, TILE), half_of),
                pl.BlockSpec((hidden, count), lambda i, core: (int(other), first // count)),
                pl.BlockSpec(rows.shape, lambda i, core: (0, 0, 0)),
            ],
            out_specs=pl.BlockSpec((hidden, count), lambda i, core: (0, 0)),
        ),
        compiler_params=params(24),
        cost_estimate=pl.CostEstimate(
            flops=hidden * planes * TILE * count,
            bytes_accessed=weights.size + 2 * rows.size,
            transcendentals=0,
        ),
    )(core, weights, slope, rows)


def place_kernel(first, *refs):
    here_ref, there_ref, here_place_ref, there_place_ref = refs[-5:-1]
    out_ref = refs[-1]
    span = slice(first, first + here_ref.shape[1])
    placed = jnp.dot(here_ref[...], here_place_ref[span, :], preferred_element_type=jnp.float32)
    placed += jnp.dot(there_ref[...], there_place_ref[span, :], preferred_element_type=jnp.float32)
    if len(refs) > 5:
        placed += refs[0][...].astype(jnp.float32)
    out_ref[...] = placed.astype(out_ref.dtype)


def put(here, there, here_place, there_place, first, base):
    hidden = here.shape[0]
    operands = base + [here, there, here_place, there_place]
    return pl.pallas_call(
        functools.partial(place_kernel, first),
        out_shape=jax.ShapeDtypeStruct((hidden, SLOTS), jnp.bfloat16),
        in_specs=[VMEM] * len(operands),
        out_specs=VMEM,
        compiler_params=params(16),
        cost_estimate=pl.CostEstimate(
            flops=4 * hidden * here.shape[1] * SLOTS,
            bytes_accessed=4 * SLOTS * here.shape[1],
            transcendentals=0,
        ),
    )(*operands)


def ring_pairs(other_core):
    pairs = []
    for z in range(16):
        for core in range(2):
            below = (z + (-1 if core == 0 else 1)) % 16
            sender = 1 - core if other_core else core
            pairs.append((below * 2 + sender, z * 2 + core))
    return pairs


def shards(grad_hidden, positions, owner_ids, w_proj, pre_act):
    zhi, zlo, core = (lax.axis_index(name) for name in ("zhi", "zlo", "core"))
    width = grad_hidden.shape[1]
    zhi_at = jnp.reshape(zhi, (1,)).astype(jnp.int32)
    core_at = jnp.reshape(core, (1,)).astype(jnp.int32)
    swap = [(0, 1), (1, 0)]

    packed = pick(grad_hidden, positions, owner_ids)

    other = lax.ppermute(w_proj, "zhi", swap)
    both = jnp.concatenate(
        [jnp.where(zhi == 0, w_proj, other), jnp.where(zhi == 0, other, w_proj)], axis=1
    )

    kept, crossed = [packed], [packed]
    for step in range(1, STEPS + 1):
        kept.append(lax.ppermute(kept[-1], RING, ring_pairs(False)))
        if step < STEPS:
            crossed.append(lax.ppermute(crossed[-1], RING, ring_pairs(step == 1)))
        if step == WEIGHTS_BY:
            kept[-1], crossed[-1], both = lax.optimization_barrier((kept[-1], crossed[-1], both))
            weights = lax.all_gather(both, ("core",) + PLANE, axis=0, tiled=False)
    chunks = [packed]
    for step in range(1, STEPS + 1):
        chunks.append(kept[step])
        if step < STEPS:
            chunks.append(crossed[step])

    pre = pre_act[0].T
    slope, here_place, there_place = slopes(
        zhi * 8 + zlo, core, pre, lax.ppermute(pre, "core", swap)
    )

    placed = []
    first = 0
    for count in GROUPS:
        outgoing = dispatch(chunks[first : first + count], zhi_at, width)
        received = lax.all_to_all(outgoing, PLANE, split_axis=0, concat_axis=0, tiled=True)
        at = (core_at, weights, slope, received, first * IMG, count * IMG)
        if first == 0:
            here, there = project(*at)
            there = lax.ppermute(there, "core", swap)
        else:
            there = lax.ppermute(project_half(*at, True), "core", swap)
            here = project_half(*at, False)
        placed = [put(here, there, here_place, there_place, first * IMG, placed)]
        first += count
    return placed[0].T[None]


def solution(mesh):
    fine = Mesh(mesh.devices.reshape(SIZES), AXES)
    return jax.shard_map(
        shards,
        mesh=fine,
        in_specs=(
            P(AXES, None),
            P(AXES),
            P(AXES, None),
            P(("zlo", "core"), ("x", "zhi", "y")),
            P(("x", "zhi", "y"), None, ("zlo", "core")),
        ),
        out_specs=P(("x", "zhi", "y"), None, ("zlo", "core")),
        check_vma=False,
    )
```
